128 devices in a mesh: wide: 16 (over x, y), eight: 8 (over z, core).
Axes of the slice: x: 4, y: 4, z: 4, core: 2. Of those that a mesh axis runs over, the one named last changes fastest.
Arguments:
- tokens: bfloat16 [16384, 2048], P(('wide', 'eight')), may hold values from -6 to 6
- grad_out: bfloat16 [16384, 2048], P(('wide', 'eight')), may hold values from -6 to 6
- routes: int32 [16384, 2], P(('wide', 'eight')), may hold values from 0 to 127, all different within a row; in each aligned block of 128 rows (0 to 127, 128 to 255, ...) at most 3 rows name the same one
- route_probs: float32 [16384, 2], P(('wide', 'eight')), may hold values from 0.1 to 1
- gate_weight: bfloat16 [128, 2048, 512], P(('wide', 'eight')), may hold values from -0.125 to 0.125
- up_weight: bfloat16 [128, 2048, 512], P(('wide', 'eight')), may hold values from -0.125 to 0.125
- down_weight: bfloat16 [128, 512, 2048], P(('wide', 'eight')), may hold values from -0.25 to 0.25
- momentum: float32 [128, 512, 2048], P(('wide', 'eight')), may hold values from -18 to 18
Outputs:
- grad_input: bfloat16 [16384, 2048], P(('wide', 'eight'))
- grad_gate: bfloat16 [128, 2048, 512], P(('wide', 'eight'))
- grad_up: bfloat16 [128, 2048, 512], P(('wide', 'eight'))
- momentum_out: float32 [128, 512, 2048], P(('wide', 'eight'))
- update: bfloat16 [128, 512, 2048], P(('wide', 'eight'))
The draws below stay inside these ranges and needn't reach their ends.
Inputs may be any that keep to these rules, and one draw needn't show every extreme that they name: `routes`: each row names 2 different experts; among the 128 tokens of one device no expert is named more than 3 times, and in some device's tokens some expert is named exactly 3 times.
All inputs are finite; a program needn't handle non-finite values.
Results may differ from the reference program's by a relative error of at most 0.015.
Values may be sent and summed in bfloat16 or wider, within the bound.
A program may use at most 128 MiB of HBM per device.

```python
import math
import jax
import jax.numpy as jnp
import numpy as np
from jax import lax

D = 2048
F = 512
TOK_DEV = 128
TOP = 2
NS_STEPS = 3
EXPERTS = 128
TOKENS = 16384
CAP = 3


def level_of(own_key, dims, shards, least, high):
    gain = 1.0
    for dim, blocks in shards:
        steps = jax.random.uniform(jax.random.fold_in(jax.random.fold_in(own_key, 6), dim), (blocks,), jnp.float32, least / len(shards), high / len(shards))
        gain = gain * jnp.repeat(jnp.exp(steps), dims[dim] // blocks).reshape((-1,) + (1,) * (len(dims) - 1 - dim))
    return gain


def routed_block(stream_key, own, number, rows, amount, top, most, lean):
    sequence = jax.random.permutation(stream_key, amount)
    crowded, ordinary = portions_of(amount, rows * top, most, lean, True), portions_of(amount, rows * top, most, lean, False)
    places = jnp.arange(amount)

    def named(sizes, offset_by):
        used = int((sizes > 0).sum())
        fixed = max(1, used // 4)
        shifted = fixed + (places - fixed + offset_by * (used - fixed)) % max(1, amount - fixed)
        return jnp.zeros((amount,), jnp.int32).at[sequence[jnp.where(places < fixed, places, shifted)]].set(jnp.asarray(sizes, jnp.int32))

    sizes = jnp.where(number % 4 == 0, named(crowded, number // 4), named(ordinary, number - number // 4 - 1))
    mixed = jax.random.permutation(jax.random.fold_in(own, 3), amount)
    giver, sink = mixed[0:amount // 2 * 2:2], mixed[1:amount // 2 * 2:2]
    margin = jnp.minimum(sizes[giver] - 1, most - sizes[sink]) // 2
    margin = jnp.where((giver == sequence[0]) | (sink == sequence[0]) | (sizes[sink] == 0), 0, jnp.maximum(margin, 0))
    shifted = jax.random.randint(jax.random.fold_in(own, 4), (amount // 2,), 0, 1 << 20) % (margin + 1)
    sizes = sizes.at[giver].add(-shifted).at[sink].add(shifted)
    members = jnp.searchsorted(jnp.cumsum(sizes), jnp.arange(rows * top), side="right").astype(jnp.int32)
    listing = members.reshape(top, rows).T
    listing = listing[jax.random.permutation(jax.random.fold_in(own, 1), rows)]
    offset_by = jax.random.randint(jax.random.fold_in(own, 2), (rows, 1), 0, top)
    return jnp.take_along_axis(listing, (jnp.arange(top)[None, :] + offset_by) % top, axis=1)


def portions_of(amount, total, reach, lean, full):
    loads = [(1 << 20) // math.isqrt(standing ** lean) + 1 for standing in range(1, amount + 1)]
    largest = reach if full else min(reach, max(-(-total // amount), total * loads[0] // sum(loads)))
    least = 1 if total - largest >= amount - 1 else 0
    given, spare = [largest] + [least] * (amount - 1), total - largest - least * (amount - 1)
    while spare > 0:
        free = [i for i in range(1, amount) if given[i] < largest] or [i for i in range(1, amount) if given[i] < reach]
        mass, budget = sum([loads[i] for i in free]), spare
        for i in free:
            more = min(reach - given[i], max(1, budget * loads[i] // mass), spare)
            given[i] = given[i] + more
            spare = spare - more
    return np.array(given)


def scatter_about(key, dims, scale, limit, shards=(), kind=jnp.bfloat16):
    values = jax.random.normal(key, dims, jnp.float32) * scale
    if len(shards) > 0:
        values = level_of(key, dims, shards, -0.22, 0.18) * values
    return jnp.clip(values, min=-limit, max=limit).astype(kind)


def setup_inputs(seed: int = 0) -> dict:
    arg_keys = jax.random.split(jax.random.key(seed), 9)
    tokens = scatter_about(arg_keys[0], (TOKENS, D), 1.0, 6.0, ((0, 128),))
    grad_out = scatter_about(arg_keys[1], (TOKENS, D), 1.0, 6.0, ((0, 128),))
    routes_keys = jax.random.split(jax.random.fold_in(arg_keys[2], 1), TOKENS // TOK_DEV)
    routes_turns = jax.random.permutation(jax.random.fold_in(arg_keys[2], 3), TOKENS // TOK_DEV)
    routes = jax.vmap(lambda own, number: routed_block(jax.random.fold_in(arg_keys[2], 2), own, number, TOK_DEV, EXPERTS, TOP, CAP, 2))(routes_keys, routes_turns).reshape((TOKENS, TOP))
    route_probs = jnp.clip(jnp.exp(math.log(1.0) - 2.3025851 * jax.random.uniform(arg_keys[3], (TOKENS, TOP), jnp.float32) ** level_of(arg_keys[3], (TOKENS, TOP), ((0, 128),), -0.2, 0.2)), 0.1, 1.0)
    gate_weight = scatter_about(arg_keys[4], (EXPERTS, D, F), D ** -0.5, 0.125, ((0, 128),))
    up_weight = scatter_about(arg_keys[5], (EXPERTS, D, F), D ** -0.5, 0.125, ((0, 128),))
    down_weight = scatter_about(arg_keys[6], (EXPERTS, F, D), F ** -0.5, 0.25, ((0, 128),))
    momentum = scatter_about(arg_keys[7], (EXPERTS, F, D), 3.0, 18.0, ((0, 128),), jnp.float32)
    return {"tokens": tokens, "grad_out": grad_out, "routes": routes, "route_probs": route_probs, "gate_weight": gate_weight, "up_weight": up_weight, "down_weight": down_weight, "momentum": momentum}


ns_coeffs = (3.4445, -4.775, 2.0315)
momentum_decay = 0.95
norm_eps = 1e-07

def silu_parts(gate_pre):
    sigmoid_gate = jax.nn.sigmoid(gate_pre)
    gate_act = gate_pre * sigmoid_gate
    gate_slope = sigmoid_gate * (1.0 + gate_pre * (1.0 - sigmoid_gate))
    return (gate_act, gate_slope)

def expert_backward(rows_input, rows_grad, gate_mat, up_mat, down_mat):
    gate_pre = jnp.dot(rows_input, gate_mat, preferred_element_type=jnp.float32)
    upper = jnp.dot(rows_input, up_mat, preferred_element_type=jnp.float32)
    gate_act, gate_slope = silu_parts(gate_pre)
    hidden = (gate_act * upper).astype(jnp.bfloat16)
    grad_hidden = jnp.dot(rows_grad, down_mat.T, preferred_element_type=jnp.float32)
    grad_gate_pre = (grad_hidden * upper * gate_slope).astype(jnp.bfloat16)
    grad_upper = (grad_hidden * gate_act).astype(jnp.bfloat16)
    grad_rows = (jnp.dot(grad_gate_pre, gate_mat.T, preferred_element_type=jnp.float32) + jnp.dot(grad_upper, up_mat.T, preferred_element_type=jnp.float32)).astype(jnp.bfloat16)
    grad_gate = jnp.dot(rows_input.T, grad_gate_pre, preferred_element_type=jnp.float32)
    grad_up = jnp.dot(rows_input.T, grad_upper, preferred_element_type=jnp.float32)
    grad_down = jnp.dot(hidden.T, rows_grad, preferred_element_type=jnp.float32)
    return (grad_rows, grad_gate, grad_up, grad_down)

def orthogonalize(ortho):
    coef_lin, coef_sq, coef_quart = ns_coeffs
    mixed = ortho.astype(jnp.float32)
    for ns_turn in range(NS_STEPS):
        square = jnp.dot(ortho, ortho.T, preferred_element_type=jnp.float32).astype(jnp.bfloat16)
        quartic = jnp.dot(square, square, preferred_element_type=jnp.float32)
        poly_term = (coef_sq * square.astype(jnp.float32) + coef_quart * quartic).astype(jnp.bfloat16)
        mixed = coef_lin * ortho.astype(jnp.float32) + jnp.dot(poly_term, ortho, preferred_element_type=jnp.float32)
        if ns_turn + 1 < NS_STEPS:
            ortho = mixed.astype(jnp.bfloat16)
    return (math.sqrt(D) * mixed).astype(jnp.bfloat16)

def reference(tokens, grad_out, routes, route_probs, gate_weight, up_weight, down_weight, momentum):
    route_ids = routes.reshape(-1).astype(jnp.int32)
    total_routes = route_ids.shape[0]
    slots = EXPERTS * CAP
    sorted_pos = jnp.argsort(route_ids, stable=True).astype(jnp.int32)
    counts = lax.optimization_barrier(jnp.sum((route_ids[None, :] == jnp.arange(EXPERTS, dtype=jnp.int32)[:, None]).astype(jnp.int32), axis=1))
    offsets = (jnp.cumsum(counts) - counts).astype(jnp.int32)
    padded_pos = jnp.concatenate([sorted_pos, jnp.zeros((slots,), jnp.int32)])
    scaled = (route_probs[:, :, None] * grad_out[:, None, :].astype(jnp.float32)).astype(jnp.bfloat16)
    scaled = scaled.reshape(total_routes, D)

    def per_expert(accumulator, inputs):
        expert, gate_mat, up_mat, down_mat, moment_old = inputs
        picked = lax.dynamic_slice(padded_pos, (offsets[expert].astype(jnp.int32),), (slots,))
        is_live = jnp.arange(slots, dtype=jnp.int32) < counts[expert]
        token_rows = (picked // TOP).astype(jnp.int32)
        rows_input = jnp.where(is_live[:, None], tokens[token_rows], jnp.zeros((), tokens.dtype))
        rows_grad = jnp.where(is_live[:, None], scaled[picked], jnp.zeros((), scaled.dtype))
        grad_rows, grad_gate, grad_up, grad_down = expert_backward(rows_input, rows_grad, gate_mat, up_mat, down_mat)
        target = jnp.where(is_live, token_rows, TOKENS).astype(jnp.int32)
        accumulator = accumulator.at[target].add(grad_rows.astype(jnp.float32), mode='drop')
        moment = momentum_decay * moment_old + grad_down
        inverse_norm = 1.0 / (jnp.sqrt(jnp.sum(moment * moment)) + norm_eps)
        ortho_start = (moment * inverse_norm).astype(jnp.bfloat16)
        update = orthogonalize(ortho_start)
        return (accumulator, (grad_gate.astype(jnp.bfloat16), grad_up.astype(jnp.bfloat16), moment, update))
    accumulator, stacked = lax.scan(per_expert, jnp.zeros((TOKENS, D), jnp.float32), (jnp.arange(EXPERTS, dtype=jnp.int32), gate_weight, up_weight, down_weight, momentum))
    grad_gate, grad_up, momentum_out, update = stacked
    return (accumulator.astype(jnp.bfloat16), grad_gate, grad_up, momentum_out, update)
```

```python
import functools
import math

import jax
import jax.numpy as jnp
from jax import lax
from jax.experimental import pallas as pl
from jax.experimental.pallas import tpu as pltpu
from jax.sharding import PartitionSpec as P

MESH = pl.DeviceIdType.MESH
BF = jnp.bfloat16
F32 = jnp.float32
NS_STEPS = 3
NS_COEFFS = (3.4445, -4.775, 2.0315)
DECAY = 0.95
NORM_EPS = 1e-07
CAP = 3
STRIDE = 37
CHUNKS = 4
LANES = 128


def axis_dims(size):
    return {16: (4, 4), 8: (4, 2)}.get(size, (size,))


def digits(value, dims):
    out = []
    for d in reversed(dims):
        out.append(lax.rem(value, d))
        value = lax.div(value, d)
    return out[::-1]


def number(parts, dims):
    value = parts[0]
    for p, d in zip(parts[1:], dims[1:]):
        value = value * d + p
    return value


def shifted(place, offset, dims, sign):
    return number(
        [lax.rem(p + d + sign * o, d) for p, o, d in zip(digits(place, dims), digits(offset, dims), dims)],
        dims,
    )


def mm(a, b):
    return lax.dot_general(a, b, (((1,), (0,)), ((), ())), preferred_element_type=F32)


def mm_nt(a, b):
    return lax.dot_general(a, b, (((1,), (1,)), ((), ())), preferred_element_type=F32)


def mm_tn(a, b):
    return lax.dot_general(a, b, (((0,), (0,)), ((), ())), preferred_element_type=F32)


def kernel(
    wide, eight,
    tok_of, prob_of, place_of, tokens, grad_out, gate_hbm, up_hbm, down_hbm, mom_hbm,
    gi_out, gg_out, gu_out, mo_out, upd_out,
    tok_f, grad_f, send, recv, back, home, tile_f, rows_x, rows_g, hid, ggp, gup,
    gate_w, up_w, down_w, mo, ortho, sq, poly, gg_v, gu_v,
    load_sem, store_sem, send_sem, recv_sem, back_sem, home_sem,
):
    n = wide * eight
    toks, width = tokens.shape
    hidden = down_w.shape[0]
    subs = width // LANES
    per = n // CHUNKS
    crows = per * CAP
    me = (lax.axis_index("wide"), lax.axis_index("eight"))
    wd, ed = axis_dims(wide), axis_dims(eight)

    def peer(block, sign):
        o = lax.rem(block * STRIDE, n)
        return (
            shifted(me[0], lax.div(o, eight), wd, sign),
            shifted(me[1], lax.rem(o, eight), ed, sign),
        )

    barrier = pltpu.get_barrier_semaphore()

    def greet(i, _):
        pl.semaphore_signal(barrier, inc=1, device_id=peer(i, 1), device_id_type=MESH)
        return 0

    lax.fori_loop(1, n, greet, 0)

    loads = [
        pltpu.make_async_copy(src, dst, load_sem.at[k])
        for k, (src, dst) in enumerate(
            [(gate_hbm, gate_w), (up_hbm, up_w), (down_hbm, down_w), (mom_hbm, mo)]
        )
    ]
    for c in loads:
        c.start()

    tok_flat, grad_flat = (r.reshape(toks * subs, LANES) for r in (tok_f, grad_f))
    for j in range(subs):
        cols = slice(j * LANES, (j + 1) * LANES)
        tok_flat[pl.ds(j, toks, stride=subs), :] = tokens[:, cols].astype(F32)
        grad_flat[pl.ds(j, toks, stride=subs), :] = grad_out[:, cols].astype(F32)

    def fill(i):
        for s in range(CAP):
            token = tok_of[i * CAP + s]
            send[i, s] = tok_f[token].astype(BF)
            send[i, CAP + s] = (prob_of[i * CAP + s] * grad_f[token]).astype(BF)

    fill(0)
    own = pltpu.make_async_copy(send.at[0], recv.at[0], recv_sem.at[0])
    own.start()

    pl.semaphore_wait(barrier, n - 1)

    def dispatch(i, _):
        fill(i)
        pltpu.make_async_remote_copy(
            src_ref=send.at[i], dst_ref=recv.at[i], send_sem=send_sem,
            recv_sem=recv_sem.at[lax.div(i, per)], device_id=peer(i, 1), device_id_type=MESH,
        ).start()
        return 0

    lax.fori_loop(1, n, dispatch, 0)

    for c in loads:
        c.wait()

    def decay(b, _):
        rows = pl.ds(pl.multiple_of(b * 64, 64), 64)
        mo[rows, :] = DECAY * mo[rows, :]
        return 0

    lax.fori_loop(0, hidden // 64, decay, 0)

    def chunk(c, _):
        blocks = pl.ds(c * per, per)
        rows = pl.ds(pl.multiple_of(c * crows, crows), crows)
        pltpu.make_async_copy(recv.at[blocks], recv.at[blocks], recv_sem.at[c]).wait()
        for part, dest in ((0, rows_x), (CAP, rows_g)):
            tile_f[...] = recv[blocks, part:part + CAP].astype(F32).reshape(crows * subs, LANES)
            for j in range(subs):
                dest[rows, j * LANES:(j + 1) * LANES] = tile_f[pl.ds(j, crows, stride=subs), :].astype(BF)
        x, g = rows_x[rows, :], rows_g[rows, :]
        gate_pre = mm(x, gate_w[...])
        upper = mm(x, up_w[...])
        grad_hidden = mm_nt(g, down_w[...])
        sig = jax.nn.sigmoid(gate_pre)
        act = gate_pre * sig
        slope = sig * (1.0 + gate_pre * (1.0 - sig))
        hid[...] = (act * upper).astype(BF)
        ggp[rows, :] = (grad_hidden * upper * slope).astype(BF)
        gup[rows, :] = (grad_hidden * act).astype(BF)
        step = 2 * LANES
        for b in range(width // step):
            cols = slice(b * step, (b + 1) * step)
            gr = mm_nt(ggp[rows, :], gate_w[cols, :]) + mm_nt(gup[rows, :], up_w[cols, :])
            tile_f[pl.ds(2 * b, crows, stride=subs), :] = gr[:, :LANES]
            tile_f[pl.ds(2 * b + 1, crows, stride=subs), :] = gr[:, LANES:]
        back[rows] = tile_f[...].astype(BF).reshape(crows, subs, LANES)

        def give(i, _):
            own_rows = pl.ds(i * CAP, CAP)

            @pl.when(i == 0)
            def _():
                pltpu.make_async_copy(back.at[own_rows], home.at[own_rows], home_sem).start()

            @pl.when(i > 0)
            def _():
                pltpu.make_async_remote_copy(
                    src_ref=back.at[own_rows], dst_ref=home.at[own_rows], send_sem=back_sem,
                    recv_sem=home_sem, device_id=peer(i, -1), device_id_type=MESH,
                ).start()

            return 0

        lax.fori_loop(c * per, (c + 1) * per, give, 0)
        step = 512
        for b in range(width // step):
            cols = slice(b * step, (b + 1) * step)
            mo[:, cols] += mm_tn(hid[...], rows_g[rows, cols])
        return 0

    lax.fori_loop(0, CHUNKS, chunk, 0)

    stores = [pltpu.make_async_copy(mo, mo_out, store_sem.at[0])]
    stores[-1].start()

    def squares(b, total):
        part = mo[pl.ds(pl.multiple_of(b * 32, 32), 32), :]
        part = part * part
        return total + jnp.sum(part.reshape(4, 8, width), axis=0)

    norm2 = jnp.sum(lax.fori_loop(0, hidden // 32, squares, jnp.zeros((8, width), F32)))
    inverse = 1.0 / (jnp.sqrt(jnp.full((8, LANES), norm2, F32)) + NORM_EPS)
    inverse = inverse[0:1, 0:1]

    def scaled(b, _):
        rows = pl.ds(pl.multiple_of(b * 64, 64), 64)
        ortho[rows, :] = (mo[rows, :] * inverse).astype(BF)
        return 0

    lax.fori_loop(0, hidden // 64, scaled, 0)

    lin, quad, quart = NS_COEFFS
    step = 512
    for turn in range(NS_STEPS):
        sq[...] = mm_nt(ortho[...], ortho[...]).astype(BF)
        poly[...] = (quad * sq[...].astype(F32) + quart * mm(sq[...], sq[...])).astype(BF)
        scale = math.sqrt(width) if turn + 1 == NS_STEPS else None
        for b in range(width // step):
            cols = slice(b * step, (b + 1) * step)
            mixed = lin * ortho[:, cols].astype(F32) + mm(poly[...], ortho[:, cols])
            ortho[:, cols] = (mixed if scale is None else scale * mixed).astype(BF)
    stores.append(pltpu.make_async_copy(ortho, upd_out, store_sem.at[1]))
    stores[-1].start()

    step = 2 * LANES

    def weight_grads(b, _):
        rows = pl.ds(pl.multiple_of(b * step, step), step)
        x = rows_x[:, rows]
        gg_v[rows, :] = mm_tn(x, ggp[...]).astype(BF)
        gu_v[rows, :] = mm_tn(x, gup[...]).astype(BF)
        return 0

    lax.fori_loop(0, width // step, weight_grads, 0)
    stores.append(pltpu.make_async_copy(gg_v, gg_out, store_sem.at[2]))
    stores[-1].start()
    stores.append(pltpu.make_async_copy(gu_v, gu_out, store_sem.at[3]))
    stores[-1].start()

    pltpu.make_async_copy(home, home, home_sem).wait()

    def combine(t, _):
        first = home[place_of[2 * t]].astype(F32)
        second = home[place_of[2 * t + 1]].astype(F32)
        tok_f[t] = first + second
        return 0

    lax.fori_loop(0, toks, combine, 0, unroll=4)
    for j in range(subs):
        gi_out[:, j * LANES:(j + 1) * LANES] = tok_flat[pl.ds(j, toks, stride=subs), :].astype(BF)

    rest = pl.ds(1, n - 1)
    pltpu.make_async_copy(send.at[rest], send.at[rest], send_sem).wait()
    rest = pl.ds(CAP, (n - 1) * CAP)
    pltpu.make_async_copy(back.at[rest], back.at[rest], back_sem).wait()
    for s in stores:
        s.wait()


def per_device(tokens, grad_out, routes, route_probs, gate_weight, up_weight, down_weight, momentum):
    wide, eight = lax.axis_size("wide"), lax.axis_size("eight")
    n = wide * eight
    toks, top = routes.shape
    width = tokens.shape[1]
    hidden = down_weight.shape[1]
    subs = width // LANES
    slots = n * CAP
    total = toks * top

    ids = routes.reshape(-1)
    me = (lax.axis_index("wide"), lax.axis_index("eight"))
    wd, ed = axis_dims(wide), axis_dims(eight)

    def offset(there, here, dims):
        return number(
            [lax.rem(t - h + d, d) for t, h, d in zip(digits(there, dims), digits(here, dims), dims)],
            dims,
        )

    o = offset(lax.div(ids, eight), me[0], wd) * eight + offset(lax.rem(ids, eight), me[1], ed)
    block = lax.rem(o * pow(STRIDE, -1, n), n)
    order = jnp.arange(total, dtype=jnp.int32)
    earlier = (ids[:, None] == ids[None, :]) & (order[None, :] < order[:, None])
    place = block * CAP + jnp.sum(earlier.astype(jnp.int32), axis=1)
    match = place[None, :] == jnp.arange(slots, dtype=jnp.int32)[:, None]
    tok_of = jnp.sum(jnp.where(match, order[None, :] // top, 0), axis=1)
    prob_of = jnp.sum(jnp.where(match, route_probs.reshape(-1)[None, :], 0.0), axis=1)

    smem = pl.BlockSpec(memory_space=pltpu.SMEM)
    vmem = pl.BlockSpec(memory_space=pltpu.VMEM)
    hbm = pl.BlockSpec(memory_space=pl.ANY)
    outs = pl.pallas_call(
        functools.partial(kernel, wide, eight),
        out_shape=(
            jax.ShapeDtypeStruct((toks, width), BF),
            jax.ShapeDtypeStruct((width, hidden), BF),
            jax.ShapeDtypeStruct((width, hidden), BF),
            jax.ShapeDtypeStruct((hidden, width), F32),
            jax.ShapeDtypeStruct((hidden, width), BF),
        ),
        in_specs=[smem] * 3 + [vmem] * 2 + [hbm] * 4,
        out_specs=(vmem, hbm, hbm, hbm, hbm),
        scratch_shapes=[
            pltpu.VMEM((toks, subs, LANES), F32),
            pltpu.VMEM((toks, subs, LANES), F32),
            pltpu.VMEM((n, 2 * CAP, subs, LANES), BF),
            pltpu.VMEM((n, 2 * CAP, subs, LANES), BF),
            pltpu.VMEM((slots, subs, LANES), BF),
            pltpu.VMEM((slots, subs, LANES), BF),
            pltpu.VMEM((slots // CHUNKS * subs, LANES), F32),
            pltpu.VMEM((slots, width), BF),
            pltpu.VMEM((slots, width), BF),
            pltpu.VMEM((slots // CHUNKS, hidden), BF),
            pltpu.VMEM((slots, hidden), BF),
            pltpu.VMEM((slots, hidden), BF),
            pltpu.VMEM((width, hidden), BF),
            pltpu.VMEM((width, hidden), BF),
            pltpu.VMEM((hidden, width), BF),
            pltpu.VMEM((hidden, width), F32),
            pltpu.VMEM((hidden, width), BF),
            pltpu.VMEM((hidden, hidden), BF),
            pltpu.VMEM((hidden, hidden), BF),
            pltpu.VMEM((width, hidden), BF),
            pltpu.VMEM((width, hidden), BF),
            pltpu.SemaphoreType.DMA((4,)),
            pltpu.SemaphoreType.DMA((4,)),
            pltpu.SemaphoreType.DMA,
            pltpu.SemaphoreType.DMA((CHUNKS,)),
            pltpu.SemaphoreType.DMA,
            pltpu.SemaphoreType.DMA,
        ],
        compiler_params=pltpu.CompilerParams(
            collective_id=0, has_side_effects=True, vmem_limit_bytes=58 * 2**20
        ),
        name="experts",
    )(
        tok_of, prob_of, place, tokens, grad_out,
        gate_weight[0], up_weight[0], down_weight[0], momentum[0],
    )
    gi, gg, gu, mo, upd = outs
    return gi, gg[None], gu[None], mo[None], upd[None]


def solution(mesh):
    flat, deep = P(("wide", "eight"), None), P(("wide", "eight"), None, None)
    return jax.shard_map(
        per_device,
        mesh=mesh,
        in_specs=(flat,) * 4 + (deep,) * 4,
        out_specs=(flat,) + (deep,) * 4,
        check_vma=False,
    )
```

```python
import functools
import math

import jax
import jax.numpy as jnp
from jax import lax
from jax.experimental import pallas as pl
from jax.experimental.pallas import tpu as pltpu
from jax.sharding import PartitionSpec as P

MESH = pl.DeviceIdType.MESH
BF = jnp.bfloat16
F32 = jnp.float32
NS_STEPS = 3
NS_COEFFS = (3.4445, -4.775, 2.0315)
DECAY = 0.95
NORM_EPS = 1e-07
CAP = 3
STRIDE = 37
CHUNKS = 4
LANES = 128


def axis_dims(size):
    return {16: (4, 4), 8: (4, 2)}.get(size, (size,))


def digits(value, dims):
    out = []
    for d in reversed(dims):
        out.append(lax.rem(value, d))
        value = lax.div(value, d)
    return out[::-1]


def number(parts, dims):
    value = parts[0]
    for p, d in zip(parts[1:], dims[1:]):
        value = value * d + p
    return value


def shifted(place, offset, dims, sign):
    return number(
        [lax.rem(p + d + sign * o, d) for p, o, d in zip(digits(place, dims), digits(offset, dims), dims)],
        dims,
    )


def mm(a, b):
    return lax.dot_general(a, b, (((1,), (0,)), ((), ())), preferred_element_type=F32)


def mm_nt(a, b):
    return lax.dot_general(a, b, (((1,), (1,)), ((), ())), preferred_element_type=F32)


def mm_tn(a, b):
    return lax.dot_general(a, b, (((0,), (0,)), ((), ())), preferred_element_type=F32)


def kernel(
    wide, eight,
    routes, probs, tok_hbm, grad_hbm, gate_hbm, up_hbm, down_hbm, mom_hbm,
    place_out, home, mo, ortho, gg_v, gu_v,
    tokens, grad_out, tok_v, prob_v, tok_of, prob_of,
    tok_f, grad_f, send, recv, back, tile_f, rows_x, rows_g, hid, ggp, gup,
    gate_w, up_w, down_w, sq, poly,
    load_sem, send_sem, recv_sem, back_sem, home_sem, plane_sem, cube_sem,
):
    n = wide * eight
    toks, width = tokens.shape
    hidden = down_w.shape[0]
    subs = width // LANES
    per = n // CHUNKS
    crows = per * CAP
    me = (lax.axis_index("wide"), lax.axis_index("eight"))
    wd, ed = axis_dims(wide), axis_dims(eight)

    def peer(block, sign):
        o = lax.rem(block * STRIDE, n)
        return (
            shifted(me[0], lax.div(o, eight), wd, sign),
            shifted(me[1], lax.rem(o, eight), ed, sign),
        )

    barrier = pltpu.get_barrier_semaphore()
    row, col = wd if len(wd) == 2 else (1, wd[0])
    x, y = lax.div(me[0], col), lax.rem(me[0], col)
    xs = [(lax.rem(x + k, row) * col + y, me[1]) for k in range(1, row)]
    ys = [(x * col + lax.rem(y + k, col), me[1]) for k in range(1, col)]
    zs = [(me[0], lax.rem(me[1] + k, eight)) for k in range(1, eight)]
    for there in xs + ys + zs:
        pl.semaphore_signal(barrier, inc=1, device_id=there, device_id_type=MESH)

    loads = [
        pltpu.make_async_copy(src, dst, load_sem.at[k])
        for k, (src, dst) in enumerate(
            [
                (tok_hbm, tokens), (grad_hbm, grad_out),
                (gate_hbm, gate_w), (up_hbm, up_w), (down_hbm, down_w), (mom_hbm, mo),
            ]
        )
    ]
    for c in loads:
        c.start()

    def block_of(e):
        there = (e >> (eight.bit_length() - 1), e & (eight - 1))
        o, shift = jnp.zeros_like(e), 0
        for part, here, dims in zip(there[::-1], me[::-1], (ed, wd)):
            for d, h in zip(dims[::-1], digits(here, dims)[::-1]):
                o = o + (((part + (d - h)) & (d - 1)) << shift)
                shift += d.bit_length() - 1
                part = part >> (d.bit_length() - 1)
        return (o * pow(STRIDE, -1, n)) & (n - 1)

    def down(line):
        return jnp.broadcast_to(line, (toks, toks)).T

    sub = lax.broadcasted_iota(jnp.int32, (toks, toks), 0)
    lane = lax.broadcasted_iota(jnp.int32, (toks, toks), 1)
    e0, e1 = routes[0:1, :], routes[1:2, :]
    c0, c1 = down(e0), down(e1)

    def count(mask):
        return jnp.sum(jnp.where(mask, 1, 0), axis=0, keepdims=True)

    rank0 = count((c0 == e0) & (sub < lane))
    rank1 = count(c0 == e1) + count((c1 == e1) & (sub < lane))
    b0, b1 = block_of(e0), block_of(e1)
    place_out[0:1, :] = b0 * CAP + rank0
    place_out[1:2, :] = b1 * CAP + rank1
    p0, p1 = down(rank0 * n + b0), down(rank1 * n + b1)
    w0, w1 = down(probs[0:1, :]), down(probs[1:2, :])
    if n != toks:
        p0, p1, w0, w1 = (jnp.broadcast_to(v[:, :1], (toks, n)) for v in (p0, p1, w0, w1))
    sub = lax.broadcasted_iota(jnp.int32, (toks, n), 0)
    lane = lax.broadcasted_iota(jnp.int32, (toks, n), 1)
    for s in range(CAP):
        m0, m1 = p0 == lane + s * n, p1 == lane + s * n
        tok_v[s:s + 1, :] = jnp.sum(jnp.where(m0 | m1, sub, 0), axis=0, keepdims=True)
        prob_v[s:s + 1, :] = jnp.sum(
            jnp.where(m0, w0, 0.0) + jnp.where(m1, w1, 0.0), axis=0, keepdims=True
        )
    maps = [
        pltpu.make_async_copy(src, dst, load_sem.at[len(loads) + k])
        for k, (src, dst) in enumerate([(tok_v, tok_of), (prob_v, prob_of)])
    ]
    for c in maps:
        c.start()

    pl.semaphore_wait(barrier, len(xs + ys + zs))
    for there in ys:
        pl.semaphore_signal(plane_sem, inc=1, device_id=there, device_id_type=MESH)
    loads[0].wait()
    loads[1].wait()

    tok_flat, grad_flat = (r.reshape(toks * subs, LANES) for r in (tok_f, grad_f))
    for j in range(subs):
        cols = slice(j * LANES, (j + 1) * LANES)
        tok_flat[pl.ds(j, toks, stride=subs), :] = tokens[:, cols].astype(F32)
        grad_flat[pl.ds(j, toks, stride=subs), :] = grad_out[:, cols].astype(F32)

    def fill(i):
        for s in range(CAP):
            token = tok_of[s, i]
            send[i, s] = tok_f[token].astype(BF)
            send[i, CAP + s] = (prob_of[s, i] * grad_f[token]).astype(BF)

    pl.semaphore_wait(plane_sem, len(ys))
    for there in zs:
        pl.semaphore_signal(cube_sem, inc=1, device_id=there, device_id_type=MESH)
    for c in maps:
        c.wait()
    fill(0)
    own = pltpu.make_async_copy(send.at[0], recv.at[0], recv_sem.at[0])
    own.start()

    pl.semaphore_wait(cube_sem, len(zs))

    def dispatch(i, _):
        fill(i)
        pltpu.make_async_remote_copy(
            src_ref=send.at[i], dst_ref=recv.at[i], send_sem=send_sem,
            recv_sem=recv_sem.at[lax.div(i, per)], device_id=peer(i, 1), device_id_type=MESH,
        ).start()
        return 0

    lax.fori_loop(1, n, dispatch, 0)

    for c in loads[2:]:
        c.wait()

    def decay(b, _):
        rows = pl.ds(pl.multiple_of(b * 64, 64), 64)
        mo[rows, :] = DECAY * mo[rows, :]
        return 0

    lax.fori_loop(0, hidden // 64, decay, 0)

    def chunk(c, _):
        blocks = pl.ds(c * per, per)
        rows = pl.ds(pl.multiple_of(c * crows, crows), crows)
        pltpu.make_async_copy(recv.at[blocks], recv.at[blocks], recv_sem.at[c]).wait()
        for part, dest in ((0, rows_x), (CAP, rows_g)):
            tile_f[...] = recv[blocks, part:part + CAP].astype(F32).reshape(crows * subs, LANES)
            for j in range(subs):
                dest[rows, j * LANES:(j + 1) * LANES] = tile_f[pl.ds(j, crows, stride=subs), :].astype(BF)
        x, g = rows_x[rows, :], rows_g[rows, :]
        gate_pre = mm(x, gate_w[...])
        upper = mm(x, up_w[...])
        grad_hidden = mm_nt(g, down_w[...])
        sig = jax.nn.sigmoid(gate_pre)
        act = gate_pre * sig
        slope = sig * (1.0 + gate_pre * (1.0 - sig))
        hid[...] = (act * upper).astype(BF)
        ggp[rows, :] = (grad_hidden * upper * slope).astype(BF)
        gup[rows, :] = (grad_hidden * act).astype(BF)
        step = 2 * LANES
        for b in range(width // step):
            cols = slice(b * step, (b + 1) * step)
            gr = mm_nt(ggp[rows, :], gate_w[cols, :]) + mm_nt(gup[rows, :], up_w[cols, :])
            tile_f[pl.ds(2 * b, crows, stride=subs), :] = gr[:, :LANES]
            tile_f[pl.ds(2 * b + 1, crows, stride=subs), :] = gr[:, LANES:]
        back[rows] = tile_f[...].astype(BF).reshape(crows, subs, LANES)

        def give(i, _):
            own_rows = pl.ds(i * CAP, CAP)

            @pl.when(i == 0)
            def _():
                pltpu.make_async_copy(back.at[own_rows], home.at[own_rows], home_sem).start()

            @pl.when(i > 0)
            def _():
                pltpu.make_async_remote_copy(
                    src_ref=back.at[own_rows], dst_ref=home.at[own_rows], send_sem=back_sem,
                    recv_sem=home_sem, device_id=peer(i, -1), device_id_type=MESH,
                ).start()

            return 0

        lax.fori_loop(c * per, (c + 1) * per, give, 0)
        step = 512
        for b in range(width // step):
            cols = slice(b * step, (b + 1) * step)
            mo[:, cols] += mm_tn(hid[...], rows_g[rows, cols])
        return 0

    lax.fori_loop(0, CHUNKS, chunk, 0)

    def squares(b, total):
        part = mo[pl.ds(pl.multiple_of(b * 32, 32), 32), :]
        part = part * part
        return total + jnp.sum(part.reshape(4, 8, width), axis=0)

    norm2 = jnp.sum(lax.fori_loop(0, hidden // 32, squares, jnp.zeros((8, width), F32)))
    inverse = 1.0 / (jnp.sqrt(jnp.full((8, LANES), norm2, F32)) + NORM_EPS)
    inverse = inverse[0:1, 0:1]

    def scaled(b, _):
        rows = pl.ds(pl.multiple_of(b * 64, 64), 64)
        ortho[rows, :] = (mo[rows, :] * inverse).astype(BF)
        return 0

    lax.fori_loop(0, hidden // 64, scaled, 0)

    lin, quad, quart = NS_COEFFS
    step = 512
    for turn in range(NS_STEPS):
        sq[...] = mm_nt(ortho[...], ortho[...]).astype(BF)
        poly[...] = (quad * sq[...].astype(F32) + quart * mm(sq[...], sq[...])).astype(BF)
        scale = math.sqrt(width) if turn + 1 == NS_STEPS else None
        for b in range(width // step):
            cols = slice(b * step, (b + 1) * step)
            mixed = lin * ortho[:, cols].astype(F32) + mm(poly[...], ortho[:, cols])
            ortho[:, cols] = (mixed if scale is None else scale * mixed).astype(BF)

    step = 2 * LANES

    def weight_grads(b, _):
        rows = pl.ds(pl.multiple_of(b * step, step), step)
        x = rows_x[:, rows]
        gg_v[rows, :] = mm_tn(x, ggp[...]).astype(BF)
        gu_v[rows, :] = mm_tn(x, gup[...]).astype(BF)
        return 0

    lax.fori_loop(0, width // step, weight_grads, 0)
    pltpu.make_async_copy(home, home, home_sem).wait()
    rest = pl.ds(1, n - 1)
    pltpu.make_async_copy(send.at[rest], send.at[rest], send_sem).wait()
    rest = pl.ds(CAP, (n - 1) * CAP)
    pltpu.make_async_copy(back.at[rest], back.at[rest], back_sem).wait()


def finish(
    place_of, home, mo, ortho, gg_v, gu_v,
    gi_out, gg_out, gu_out, mo_out, upd_out,
    sums, store_sem,
):
    toks, subs, _ = sums.shape
    stores = [
        pltpu.make_async_copy(src, dst, store_sem.at[k])
        for k, (src, dst) in enumerate([(mo, mo_out), (ortho, upd_out), (gg_v, gg_out), (gu_v, gu_out)])
    ]
    for s in stores:
        s.start()

    def combine(t, _):
        sums[t] = home[place_of[0, t]].astype(F32) + home[place_of[1, t]].astype(F32)
        return 0

    lax.fori_loop(0, toks, combine, 0, unroll=4)
    flat = sums.reshape(toks * subs, LANES)
    for j in range(subs):
        gi_out[:, j * LANES:(j + 1) * LANES] = flat[pl.ds(j, toks, stride=subs), :].astype(BF)
    for s in stores:
        s.wait()


def per_device(tokens, grad_out, routes, route_probs, gate_weight, up_weight, down_weight, momentum):
    wide, eight = lax.axis_size("wide"), lax.axis_size("eight")
    n = wide * eight
    toks = routes.shape[0]
    width = tokens.shape[1]
    hidden = down_weight.shape[1]
    subs = width // LANES
    slots = n * CAP
    smem = pl.BlockSpec(memory_space=pltpu.SMEM)
    vmem = pl.BlockSpec(memory_space=pltpu.VMEM)
    hbm = pl.BlockSpec(memory_space=pl.ANY)
    kept = pl.pallas_call(
        functools.partial(kernel, wide, eight),
        out_shape=(
            jax.ShapeDtypeStruct((8, toks), jnp.int32),
            pltpu.VMEM((slots, subs, LANES), BF),
            pltpu.VMEM((hidden, width), F32),
            pltpu.VMEM((hidden, width), BF),
            pltpu.VMEM((width, hidden), BF),
            pltpu.VMEM((width, hidden), BF),
        ),
        in_specs=[vmem] * 2 + [hbm] * 6,
        out_specs=(vmem,) * 6,
        scratch_shapes=[
            pltpu.VMEM((toks, width), BF),
            pltpu.VMEM((toks, width), BF),
            pltpu.VMEM((8, n), jnp.int32),
            pltpu.VMEM((8, n), F32),
            pltpu.SMEM((8, n), jnp.int32),
            pltpu.SMEM((8, n), F32),
            pltpu.VMEM((toks, subs, LANES), F32),
            pltpu.VMEM((toks, subs, LANES), F32),
            pltpu.VMEM((n, 2 * CAP, subs, LANES), BF),
            pltpu.VMEM((n, 2 * CAP, subs, LANES), BF),
            pltpu.VMEM((slots, subs, LANES), BF),
            pltpu.VMEM((slots // CHUNKS * subs, LANES), F32),
            pltpu.VMEM((slots, width), BF),
            pltpu.VMEM((slots, width), BF),
            pltpu.VMEM((slots // CHUNKS, hidden), BF),
            pltpu.VMEM((slots, hidden), BF),
            pltpu.VMEM((slots, hidden), BF),
            pltpu.VMEM((width, hidden), BF),
            pltpu.VMEM((width, hidden), BF),
            pltpu.VMEM((hidden, width), BF),
            pltpu.VMEM((hidden, hidden), BF),
            pltpu.VMEM((hidden, hidden), BF),
            pltpu.SemaphoreType.DMA((8,)),
            pltpu.SemaphoreType.DMA,
            pltpu.SemaphoreType.DMA((CHUNKS,)),
            pltpu.SemaphoreType.DMA,
            pltpu.SemaphoreType.DMA,
            pltpu.SemaphoreType.REGULAR,
            pltpu.SemaphoreType.REGULAR,
        ],
        compiler_params=pltpu.CompilerParams(
            collective_id=0, has_side_effects=True, vmem_limit_bytes=40 * 2**20
        ),
        name="experts",
    )(
        routes.T, route_probs.T, tokens, grad_out,
        gate_weight[0], up_weight[0], down_weight[0], momentum[0],
    )
    gi, gg, gu, mo, upd = pl.pallas_call(
        finish,
        out_shape=(
            jax.ShapeDtypeStruct((toks, width), BF),
            jax.ShapeDtypeStruct((width, hidden), BF),
            jax.ShapeDtypeStruct((width, hidden), BF),
            jax.ShapeDtypeStruct((hidden, width), F32),
            jax.ShapeDtypeStruct((hidden, width), BF),
        ),
        in_specs=[smem] + [vmem] * 5,
        out_specs=(vmem, hbm, hbm, hbm, hbm),
        scratch_shapes=[
            pltpu.VMEM((toks, subs, LANES), F32),
            pltpu.SemaphoreType.DMA((4,)),
        ],
        compiler_params=pltpu.CompilerParams(vmem_limit_bytes=16 * 2**20),
        name="finish",
    )(*kept)
    return gi, gg[None], gu[None], mo[None], upd[None]


def solution(mesh):
    flat, deep = P(("wide", "eight"), None), P(("wide", "eight"), None, None)
    return jax.shard_map(
        per_device,
        mesh=mesh,
        in_specs=(flat,) * 4 + (deep,) * 4,
        out_specs=(flat,) + (deep,) * 4,
        check_vma=False,
    )
```

```python
import functools
import math

import jax
import jax.numpy as jnp
from jax import lax
from jax.experimental import pallas as pl
from jax.experimental.pallas import tpu as pltpu
from jax.sharding import PartitionSpec as P

MESH = pl.DeviceIdType.MESH
BF = jnp.bfloat16
F32 = jnp.float32
NS_STEPS = 3
NS_COEFFS = (3.4445, -4.775, 2.0315)
DECAY = 0.95
NORM_EPS = 1e-07
CAP = 3
STEPS = (2, 3)
CHUNKS = 4
PIECES = 4
LANES = 128


def axis_dims(size):
    return {16: (4, 4), 8: (4, 2)}.get(size, (size,))


def digits(value, dims):
    out = []
    for d in reversed(dims):
        out.append(lax.rem(value, d))
        value = lax.div(value, d)
    return out[::-1]


def number(parts, dims):
    value = parts[0]
    for p, d in zip(parts[1:], dims[1:]):
        value = value * d + p
    return value


def shifted(place, offset, dims, sign):
    return number(
        [lax.rem(p + d + sign * o, d) for p, o, d in zip(digits(place, dims), digits(offset, dims), dims)],
        dims,
    )


def offset_of(block, wide, eight):
    far = jnp.maximum(block - (wide + eight - 1), 0)
    q = jnp.where(block < wide, block, 0)
    r = jnp.where(block < wide, 0, block - (wide - 1))
    rest = block > wide + eight - 2
    return (
        jnp.where(rest, 1 + lax.rem(far * STEPS[0], wide - 1), q),
        jnp.where(rest, 1 + lax.rem(far * STEPS[1], eight - 1), r),
    )


def block_at(q, r, wide, eight):
    w, e = wide - 1, eight - 1
    cq = pow(STEPS[0], -1, w) * e * pow(e, -1, w) % (w * e)
    cr = pow(STEPS[1], -1, e) * w * pow(w, -1, e) % (w * e)
    far = cq * (q - 1) + cr * (r - 1)
    far = far - ((far * ((1 << 18) // (w * e) + 1)) >> 18) * (w * e)
    return jnp.where(r == 0, q, jnp.where(q == 0, wide - 1 + r, wide + eight - 1 + far))


def mm(a, b):
    return lax.dot_general(a, b, (((1,), (0,)), ((), ())), preferred_element_type=F32)


def mm_nt(a, b):
    return lax.dot_general(a, b, (((1,), (1,)), ((), ())), preferred_element_type=F32)


def mm_tn(a, b):
    return lax.dot_general(a, b, (((0,), (0,)), ((), ())), preferred_element_type=F32)


def kernel(
    wide, eight,
    routes_hbm, probs_hbm, tok_hbm, grad_hbm, gate_hbm, up_hbm, down_hbm, mom_hbm,
    place_out, home, mo, ortho, gg_v, gu_v,
    routes, probs, tokens, grad_out, tok_v, prob_v, tok_of, prob_of,
    tok_f, grad_f, send, recv, back, tile_f, rows_x, rows_g, hid, ggp, gup,
    gate_w, up_w, down_w, sq, poly,
    load_sem, send_sem, recv_sem, back_sem, home_sem, plane_sem,
):
    n = wide * eight
    toks, width = tokens.shape
    hidden = down_w.shape[0]
    subs = width // LANES
    per = n // CHUNKS
    crows = per * CAP
    me = (lax.axis_index("wide"), lax.axis_index("eight"))
    wd, ed = axis_dims(wide), axis_dims(eight)

    core = lax.rem(me[1], 2)

    def sent_to(block):
        q, r = offset_of(block, wide, eight)
        sign = 1 - 2 * core
        return shifted(me[0], q, wd, sign), shifted(me[1], r, ed, sign)

    def came_from(block):
        q, r = offset_of(block, wide, eight)
        sign = 2 * lax.rem(core + r, 2) - 1
        return shifted(me[0], q, wd, sign), shifted(me[1], r, ed, sign)

    barrier = pltpu.get_barrier_semaphore()
    near = wide + eight - 1

    def greet(i, _):
        pl.semaphore_signal(barrier, inc=1, device_id=sent_to(i), device_id_type=MESH)
        return 0

    lax.fori_loop(1, near, greet, 0)

    loads = [
        pltpu.make_async_copy(src, dst, load_sem.at[k])
        for k, (src, dst) in enumerate(
            [
                (routes_hbm, routes), (probs_hbm, probs), (tok_hbm, tokens), (grad_hbm, grad_out),
                (gate_hbm, gate_w), (up_hbm, up_w), (down_hbm, down_w), (mom_hbm, mo),
            ]
        )
    ]
    for c in loads:
        c.start()

    loads[0].wait()
    loads[1].wait()

    def block_of(e):
        there = (e >> (eight.bit_length() - 1), e & (eight - 1))
        parts = []
        for part, here, dims in zip(there, me, (wd, ed)):
            o, shift = jnp.zeros_like(e), 0
            for d, h in zip(dims[::-1], digits(here, dims)[::-1]):
                o = o + ((((part - h) * (1 - 2 * core)) & (d - 1)) << shift)
                shift += d.bit_length() - 1
                part = part >> (d.bit_length() - 1)
            parts.append(o)
        return block_at(*parts, wide, eight)

    def down(line):
        return jnp.broadcast_to(line, (toks, toks)).T

    sub = lax.broadcasted_iota(jnp.int32, (toks, toks), 0)
    lane = lax.broadcasted_iota(jnp.int32, (toks, toks), 1)
    e0, e1 = routes[0:1, :], routes[1:2, :]
    c0, c1 = down(e0), down(e1)

    def count(mask):
        return jnp.sum(jnp.where(mask, 1, 0), axis=0, keepdims=True)

    rank0 = count((c0 == e0) & (sub < lane))
    rank1 = count(c0 == e1) + count((c1 == e1) & (sub < lane))
    b0, b1 = block_of(e0), block_of(e1)
    place_out[0:1, :] = b0 * CAP + rank0
    place_out[1:2, :] = b1 * CAP + rank1
    p0, p1 = down(rank0 * n + b0), down(rank1 * n + b1)
    w0, w1 = down(probs[0:1, :]), down(probs[1:2, :])
    if n != toks:
        p0, p1, w0, w1 = (jnp.broadcast_to(v[:, :1], (toks, n)) for v in (p0, p1, w0, w1))
    sub = lax.broadcasted_iota(jnp.int32, (toks, n), 0)
    lane = lax.broadcasted_iota(jnp.int32, (toks, n), 1)
    for s in range(CAP):
        m0, m1 = p0 == lane + s * n, p1 == lane + s * n
        tok_v[s:s + 1, :] = jnp.sum(jnp.where(m0 | m1, sub, 0), axis=0, keepdims=True)
        prob_v[s:s + 1, :] = jnp.sum(
            jnp.where(m0, w0, 0.0) + jnp.where(m1, w1, 0.0), axis=0, keepdims=True
        )
    maps = [
        pltpu.make_async_copy(src, dst, load_sem.at[len(loads) + k])
        for k, (src, dst) in enumerate([(tok_v, tok_of), (prob_v, prob_of)])
    ]
    for c in maps:
        c.start()

    loads[2].wait()
    loads[3].wait()

    tok_flat, grad_flat = (r.reshape(toks * subs, LANES) for r in (tok_f, grad_f))
    for j in range(subs):
        cols = slice(j * LANES, (j + 1) * LANES)
        tok_flat[pl.ds(j, toks, stride=subs), :] = tokens[:, cols].astype(F32)
        grad_flat[pl.ds(j, toks, stride=subs), :] = grad_out[:, cols].astype(F32)

    def fill(i):
        for s in range(CAP):
            token = tok_of[s, i]
            send[i, s] = tok_f[token].astype(BF)
            send[i, CAP + s] = (prob_of[s, i] * grad_f[token]).astype(BF)

    for c in maps:
        c.wait()
    fill(0)
    own = pltpu.make_async_copy(send.at[0], recv.at[0], recv_sem.at[0])
    own.start()

    pl.semaphore_wait(barrier, near - 1)

    def tell(i, _):
        pl.semaphore_signal(plane_sem, inc=1, device_id=sent_to(i), device_id_type=MESH)
        return 0

    lax.fori_loop(wide, near, tell, 0)

    def dispatch(i, _):
        fill(i)
        pltpu.make_async_remote_copy(
            src_ref=send.at[i], dst_ref=recv.at[i], send_sem=send_sem,
            recv_sem=recv_sem.at[lax.div(i, per)], device_id=sent_to(i), device_id_type=MESH,
        ).start()
        return 0

    lax.fori_loop(1, near, dispatch, 0)
    pl.semaphore_wait(plane_sem, eight - 1)
    lax.fori_loop(near, n, dispatch, 0)

    for c in loads[4:]:
        c.wait()

    def decay(b, _):
        rows = pl.ds(pl.multiple_of(b * 64, 64), 64)
        mo[rows, :] = DECAY * mo[rows, :]
        return 0

    lax.fori_loop(0, hidden // 64, decay, 0)

    def chunk(c, _):
        blocks = pl.ds(c * per, per)
        rows = pl.ds(pl.multiple_of(c * crows, crows), crows)
        pltpu.make_async_copy(recv.at[blocks], recv.at[blocks], recv_sem.at[c]).wait()
        for part, dest in ((0, rows_x), (CAP, rows_g)):
            tile_f[...] = recv[blocks, part:part + CAP].astype(F32).reshape(crows * subs, LANES)
            for j in range(subs):
                dest[rows, j * LANES:(j + 1) * LANES] = tile_f[pl.ds(j, crows, stride=subs), :].astype(BF)
        x, g = rows_x[rows, :], rows_g[rows, :]
        gate_pre = mm(x, gate_w[...])
        upper = mm(x, up_w[...])
        grad_hidden = mm_nt(g, down_w[...])
        sig = jax.nn.sigmoid(gate_pre)
        act = gate_pre * sig
        slope = sig * (1.0 + gate_pre * (1.0 - sig))
        hid[...] = (act * upper).astype(BF)
        ggp[rows, :] = (grad_hidden * upper * slope).astype(BF)
        gup[rows, :] = (grad_hidden * act).astype(BF)
        step = 2 * LANES
        for b in range(width // step):
            cols = slice(b * step, (b + 1) * step)
            gr = mm_nt(ggp[rows, :], gate_w[cols, :]) + mm_nt(gup[rows, :], up_w[cols, :])
            tile_f[pl.ds(2 * b, crows, stride=subs), :] = gr[:, :LANES]
            tile_f[pl.ds(2 * b + 1, crows, stride=subs), :] = gr[:, LANES:]
        back[rows] = tile_f[...].astype(BF).reshape(crows, subs, LANES)

        def give(i, _):
            own_rows = pl.ds(i * CAP, CAP)

            @pl.when(i == 0)
            def _():
                pltpu.make_async_copy(back.at[own_rows], home.at[own_rows], home_sem).start()

            @pl.when(i > 0)
            def _():
                pltpu.make_async_remote_copy(
                    src_ref=back.at[own_rows], dst_ref=home.at[own_rows], send_sem=back_sem,
                    recv_sem=home_sem, device_id=came_from(i), device_id_type=MESH,
                ).start()

            return 0

        lax.fori_loop(c * per, (c + 1) * per, give, 0)
        step = 512
        for b in range(width // step):
            cols = slice(b * step, (b + 1) * step)
            mo[:, cols] += mm_tn(hid[...], rows_g[rows, cols])
        return 0

    lax.fori_loop(0, CHUNKS, chunk, 0)

    def squares(b, total):
        part = mo[pl.ds(pl.multiple_of(b * 32, 32), 32), :]
        part = part * part
        return total + jnp.sum(part.reshape(4, 8, width), axis=0)

    norm2 = jnp.sum(lax.fori_loop(0, hidden // 32, squares, jnp.zeros((8, width), F32)))
    inverse = 1.0 / (jnp.sqrt(jnp.full((8, LANES), norm2, F32)) + NORM_EPS)
    inverse = inverse[0:1, 0:1]

    def scaled(b, _):
        rows = pl.ds(pl.multiple_of(b * 64, 64), 64)
        ortho[rows, :] = (mo[rows, :] * inverse).astype(BF)
        return 0

    lax.fori_loop(0, hidden // 64, scaled, 0)

    lin, quad, quart = NS_COEFFS
    step = 512
    for turn in range(NS_STEPS):
        sq[...] = mm_nt(ortho[...], ortho[...]).astype(BF)
        poly[...] = (quad * sq[...].astype(F32) + quart * mm(sq[...], sq[...])).astype(BF)
        scale = math.sqrt(width) if turn + 1 == NS_STEPS else None
        for b in range(width // step):
            cols = slice(b * step, (b + 1) * step)
            mixed = lin * ortho[:, cols].astype(F32) + mm(poly[...], ortho[:, cols])
            ortho[:, cols] = (mixed if scale is None else scale * mixed).astype(BF)

    step = 2 * LANES

    def weight_grads(b, _):
        rows = pl.ds(pl.multiple_of(b * step, step), step)
        x = rows_x[:, rows]
        gg_v[rows, :] = mm_tn(x, ggp[...]).astype(BF)
        gu_v[rows, :] = mm_tn(x, gup[...]).astype(BF)
        return 0

    lax.fori_loop(0, width // step, weight_grads, 0)
    pltpu.make_async_copy(home, home, home_sem).wait()
    rest = pl.ds(1, n - 1)
    pltpu.make_async_copy(send.at[rest], send.at[rest], send_sem).wait()
    rest = pl.ds(CAP, (n - 1) * CAP)
    pltpu.make_async_copy(back.at[rest], back.at[rest], back_sem).wait()


def finish(
    place, home, mo, ortho, gg_v, gu_v,
    gi_out, gg_out, gu_out, mo_out, upd_out,
    place_of, sums, gi, store_sem, place_sem,
):
    toks, subs, _ = sums.shape
    plan = pltpu.make_async_copy(place, place_of, place_sem)
    plan.start()
    stores = []
    for k, (src, dst) in enumerate([(mo, mo_out), (ortho, upd_out), (gg_v, gg_out), (gu_v, gu_out)]):
        part = src.shape[0] // PIECES
        for p in range(PIECES):
            rows = pl.ds(p * part, part)
            stores.append(pltpu.make_async_copy(src.at[rows], dst.at[rows], store_sem.at[k * PIECES + p]))
            stores[-1].start()
    plan.wait()

    def combine(t, _):
        sums[t] = home[place_of[0, t]].astype(F32) + home[place_of[1, t]].astype(F32)
        return 0

    lax.fori_loop(0, toks, combine, 0, unroll=4)
    flat = sums.reshape(toks * subs, LANES)
    for j in range(subs):
        gi[:, j * LANES:(j + 1) * LANES] = flat[pl.ds(j, toks, stride=subs), :].astype(BF)
    stores.append(pltpu.make_async_copy(gi, gi_out, store_sem.at[4 * PIECES]))
    stores[-1].start()
    for s in stores:
        s.wait()


def per_device(tokens, grad_out, routes, route_probs, gate_weight, up_weight, down_weight, momentum):
    wide, eight = lax.axis_size("wide"), lax.axis_size("eight")
    n = wide * eight
    toks = routes.shape[0]
    width = tokens.shape[1]
    hidden = down_weight.shape[1]
    subs = width // LANES
    slots = n * CAP
    vmem = pl.BlockSpec(memory_space=pltpu.VMEM)
    hbm = pl.BlockSpec(memory_space=pl.ANY)
    kept = pl.pallas_call(
        functools.partial(kernel, wide, eight),
        out_shape=(
            jax.ShapeDtypeStruct((8, toks), jnp.int32),
            pltpu.VMEM((slots, subs, LANES), BF),
            pltpu.VMEM((hidden, width), F32),
            pltpu.VMEM((hidden, width), BF),
            pltpu.VMEM((width, hidden), BF),
            pltpu.VMEM((width, hidden), BF),
        ),
        in_specs=[pl.BlockSpec(memory_space=pltpu.HBM)] * 8,
        out_specs=(vmem,) * 6,
        scratch_shapes=[
            pltpu.VMEM((2, toks), jnp.int32),
            pltpu.VMEM((2, toks), F32),
            pltpu.VMEM((toks, width), BF),
            pltpu.VMEM((toks, width), BF),
            pltpu.VMEM((8, n), jnp.int32),
            pltpu.VMEM((8, n), F32),
            pltpu.SMEM((8, n), jnp.int32),
            pltpu.SMEM((8, n), F32),
            pltpu.VMEM((toks, subs, LANES), F32),
            pltpu.VMEM((toks, subs, LANES), F32),
            pltpu.VMEM((n, 2 * CAP, subs, LANES), BF),
            pltpu.VMEM((n, 2 * CAP, subs, LANES), BF),
            pltpu.VMEM((slots, subs, LANES), BF),
            pltpu.VMEM((slots // CHUNKS * subs, LANES), F32),
            pltpu.VMEM((slots, width), BF),
            pltpu.VMEM((slots, width), BF),
            pltpu.VMEM((slots // CHUNKS, hidden), BF),
            pltpu.VMEM((slots, hidden), BF),
            pltpu.VMEM((slots, hidden), BF),
            pltpu.VMEM((width, hidden), BF),
            pltpu.VMEM((width, hidden), BF),
            pltpu.VMEM((hidden, width), BF),
            pltpu.VMEM((hidden, hidden), BF),
            pltpu.VMEM((hidden, hidden), BF),
            pltpu.SemaphoreType.DMA((10,)),
            pltpu.SemaphoreType.DMA,
            pltpu.SemaphoreType.DMA((CHUNKS,)),
            pltpu.SemaphoreType.DMA,
            pltpu.SemaphoreType.DMA,
            pltpu.SemaphoreType.REGULAR,
        ],
        compiler_params=pltpu.CompilerParams(
            collective_id=0, has_side_effects=True, vmem_limit_bytes=40 * 2**20
        ),
        name="experts",
    )(
        *(
            pltpu.with_memory_space_constraint(a, pltpu.HBM)
            for a in (
                routes.T, route_probs.T, tokens, grad_out,
                gate_weight[0], up_weight[0], down_weight[0], momentum[0],
            )
        )
    )
    gi, gg, gu, mo, upd = pl.pallas_call(
        finish,
        out_shape=(
            jax.ShapeDtypeStruct((toks, width), BF),
            jax.ShapeDtypeStruct((width, hidden), BF),
            jax.ShapeDtypeStruct((width, hidden), BF),
            jax.ShapeDtypeStruct((hidden, width), F32),
            jax.ShapeDtypeStruct((hidden, width), BF),
        ),
        in_specs=[vmem] * 6,
        out_specs=(hbm,) * 5,
        scratch_shapes=[
            pltpu.SMEM((8, toks), jnp.int32),
            pltpu.VMEM((toks, subs, LANES), F32),
            pltpu.VMEM((toks, width), BF),
            pltpu.SemaphoreType.DMA((4 * PIECES + 1,)),
            pltpu.SemaphoreType.DMA,
        ],
        compiler_params=pltpu.CompilerParams(vmem_limit_bytes=16 * 2**20),
        name="finish",
    )(*kept)
    return gi, gg[None], gu[None], mo[None], upd[None]


def solution(mesh):
    flat, deep = P(("wide", "eight"), None), P(("wide", "eight"), None, None)
    return jax.shard_map(
        per_device,
        mesh=mesh,
        in_specs=(flat,) * 4 + (deep,) * 4,
        out_specs=(flat,) + (deep,) * 4,
        check_vma=False,
    )
```

```python
import functools
import math

import jax
import jax.numpy as jnp
from jax import lax
from jax.experimental import pallas as pl
from jax.experimental.pallas import tpu as pltpu
from jax.sharding import PartitionSpec as P

MESH = pl.DeviceIdType.MESH
BF = jnp.bfloat16
F32 = jnp.float32
NS_STEPS = 3
NS_COEFFS = (3.4445, -4.775, 2.0315)
DECAY = 0.95
NORM_EPS = 1e-07
CAP = 3
STRIDE = 37
CHUNKS = 4
PIECES = 4
LANES = 128


def axis_dims(size):
    return {16: (4, 4), 8: (4, 2)}.get(size, (size,))


def digits(value, dims):
    out = []
    for d in reversed(dims):
        out.append(lax.rem(value, d))
        value = lax.div(value, d)
    return out[::-1]


def number(parts, dims):
    value = parts[0]
    for p, d in zip(parts[1:], dims[1:]):
        value = value * d + p
    return value


def shifted(place, offset, dims, sign):
    return number(
        [lax.rem(p + d + sign * o, d) for p, o, d in zip(digits(place, dims), digits(offset, dims), dims)],
        dims,
    )


def mm(a, b):
    return lax.dot_general(a, b, (((1,), (0,)), ((), ())), preferred_element_type=F32)


def mm_nt(a, b):
    return lax.dot_general(a, b, (((1,), (1,)), ((), ())), preferred_element_type=F32)


def mm_tn(a, b):
    return lax.dot_general(a, b, (((0,), (0,)), ((), ())), preferred_element_type=F32)


def kernel(
    wide, eight,
    routes_hbm, probs_hbm, tok_hbm, grad_hbm, gate_hbm, up_hbm, down_hbm, mom_hbm,
    place_out, home, mo, ortho, gg_v, gu_v,
    routes, probs, tokens, grad_out, tok_v, prob_v, tok_of, prob_of,
    tok_f, grad_f, send, recv, back, tile_f, rows_x, rows_g, hid, ggp, gup,
    gate_w, up_w, down_w, sq, poly,
    load_sem, send_sem, recv_sem, back_sem, home_sem, plane_sem,
):
    n = wide * eight
    toks, width = tokens.shape
    hidden = down_w.shape[0]
    subs = width // LANES
    per = n // CHUNKS
    crows = per * CAP
    me = (lax.axis_index("wide"), lax.axis_index("eight"))
    wd, ed = axis_dims(wide), axis_dims(eight)

    def peer(block, sign):
        o = lax.rem(block * STRIDE, n)
        return (
            shifted(me[0], lax.div(o, eight), wd, sign),
            shifted(me[1], lax.rem(o, eight), ed, sign),
        )

    def across(i):
        return lax.rem(me[0] + i, wide), me[1]

    def along(i):
        return me[0], lax.rem(me[1] + i, eight)

    loads = [
        pltpu.make_async_copy(src, dst, load_sem.at[k])
        for k, (src, dst) in enumerate(
            [
                (routes_hbm, routes), (probs_hbm, probs), (tok_hbm, tokens), (grad_hbm, grad_out),
                (gate_hbm, gate_w), (up_hbm, up_w), (down_hbm, down_w), (mom_hbm, mo),
            ]
        )
    ]
    for c in loads[:4]:
        c.start()

    barrier = pltpu.get_barrier_semaphore()
    for sem, size, there in ((barrier, wide, across), (barrier, eight, along)):
        for i in range(1, size):
            pl.semaphore_signal(sem, inc=1, device_id=there(i), device_id_type=MESH)
    for c in loads[4:]:
        c.start()

    loads[0].wait()
    loads[1].wait()

    def block_of(e):
        there = (e >> (eight.bit_length() - 1), e & (eight - 1))
        o, shift = jnp.zeros_like(e), 0
        for part, here, dims in zip(there[::-1], me[::-1], (ed, wd)):
            for d, h in zip(dims[::-1], digits(here, dims)[::-1]):
                o = o + (((part - h) & (d - 1)) << shift)
                shift += d.bit_length() - 1
                part = part >> (d.bit_length() - 1)
        return (o * pow(STRIDE, -1, n)) & (n - 1)

    def down(line):
        return jnp.broadcast_to(line, (toks, toks)).T

    sub = lax.broadcasted_iota(jnp.int32, (toks, toks), 0)
    lane = lax.broadcasted_iota(jnp.int32, (toks, toks), 1)
    e0, e1 = routes[0:1, :], routes[1:2, :]
    c0, c1 = down(e0), down(e1)

    def count(mask):
        return jnp.sum(jnp.where(mask, 1, 0), axis=0, keepdims=True)

    rank0 = count((c0 == e0) & (sub < lane))
    rank1 = count(c0 == e1) + count((c1 == e1) & (sub < lane))
    b0, b1 = block_of(e0), block_of(e1)
    place_out[0:1, :] = b0 * CAP + rank0
    place_out[1:2, :] = b1 * CAP + rank1
    p0, p1 = down(rank0 * n + b0), down(rank1 * n + b1)
    w0, w1 = down(probs[0:1, :]), down(probs[1:2, :])
    if n != toks:
        p0, p1, w0, w1 = (jnp.broadcast_to(v[:, :1], (toks, n)) for v in (p0, p1, w0, w1))
    sub = lax.broadcasted_iota(jnp.int32, (toks, n), 0)
    lane = lax.broadcasted_iota(jnp.int32, (toks, n), 1)
    for s in range(CAP):
        m0, m1 = p0 == lane + s * n, p1 == lane + s * n
        tok_v[s:s + 1, :] = jnp.sum(jnp.where(m0 | m1, sub, 0), axis=0, keepdims=True)
        prob_v[s:s + 1, :] = jnp.sum(
            jnp.where(m0, w0, 0.0) + jnp.where(m1, w1, 0.0), axis=0, keepdims=True
        )
    maps = [
        pltpu.make_async_copy(src, dst, load_sem.at[len(loads) + k])
        for k, (src, dst) in enumerate([(tok_v, tok_of), (prob_v, prob_of)])
    ]
    for c in maps:
        c.start()

    pl.semaphore_wait(barrier, wide + eight - 2)
    for i in range(1, eight):
        pl.semaphore_signal(plane_sem, inc=1, device_id=along(i), device_id_type=MESH)
    loads[2].wait()
    loads[3].wait()

    tok_flat, grad_flat = (r.reshape(toks * subs, LANES) for r in (tok_f, grad_f))
    for j in range(subs):
        cols = slice(j * LANES, (j + 1) * LANES)
        tok_flat[pl.ds(j, toks, stride=subs), :] = tokens[:, cols].astype(F32)
        grad_flat[pl.ds(j, toks, stride=subs), :] = grad_out[:, cols].astype(F32)

    def fill(i):
        for s in range(CAP):
            token = tok_of[s, i]
            send[i, s] = tok_f[token].astype(BF)
            send[i, CAP + s] = (prob_of[s, i] * grad_f[token]).astype(BF)

    for c in maps:
        c.wait()
    fill(0)
    own = pltpu.make_async_copy(send.at[0], recv.at[0], recv_sem.at[0])
    own.start()

    pl.semaphore_wait(plane_sem, eight - 1)

    def dispatch(i, _):
        fill(i)
        pltpu.make_async_remote_copy(
            src_ref=send.at[i], dst_ref=recv.at[i], send_sem=send_sem,
            recv_sem=recv_sem.at[lax.div(i, per)], device_id=peer(i, 1), device_id_type=MESH,
        ).start()
        return 0

    lax.fori_loop(1, n, dispatch, 0)

    for c in loads[4:]:
        c.wait()

    def decay(b, _):
        rows = pl.ds(pl.multiple_of(b * 64, 64), 64)
        mo[rows, :] = DECAY * mo[rows, :]
        return 0

    lax.fori_loop(0, hidden // 64, decay, 0)

    def chunk(c, _):
        blocks = pl.ds(c * per, per)
        rows = pl.ds(pl.multiple_of(c * crows, crows), crows)
        pltpu.make_async_copy(recv.at[blocks], recv.at[blocks], recv_sem.at[c]).wait()
        for part, dest in ((0, rows_x), (CAP, rows_g)):
            tile_f[...] = recv[blocks, part:part + CAP].astype(F32).reshape(crows * subs, LANES)
            for j in range(subs):
                dest[rows, j * LANES:(j + 1) * LANES] = tile_f[pl.ds(j, crows, stride=subs), :].astype(BF)
        x, g = rows_x[rows, :], rows_g[rows, :]
        gate_pre = mm(x, gate_w[...])
        upper = mm(x, up_w[...])
        grad_hidden = mm_nt(g, down_w[...])
        sig = jax.nn.sigmoid(gate_pre)
        act = gate_pre * sig
        slope = sig * (1.0 + gate_pre * (1.0 - sig))
        hid[...] = (act * upper).astype(BF)
        ggp[rows, :] = (grad_hidden * upper * slope).astype(BF)
        gup[rows, :] = (grad_hidden * act).astype(BF)
        step = 2 * LANES
        for b in range(width // step):
            cols = slice(b * step, (b + 1) * step)
            gr = mm_nt(ggp[rows, :], gate_w[cols, :]) + mm_nt(gup[rows, :], up_w[cols, :])
            tile_f[pl.ds(2 * b, crows, stride=subs), :] = gr[:, :LANES]
            tile_f[pl.ds(2 * b + 1, crows, stride=subs), :] = gr[:, LANES:]
        back[rows] = tile_f[...].astype(BF).reshape(crows, subs, LANES)

        def give(i, _):
            own_rows = pl.ds(i * CAP, CAP)

            @pl.when(i == 0)
            def _():
                pltpu.make_async_copy(back.at[own_rows], home.at[own_rows], home_sem).start()

            @pl.when(i > 0)
            def _():
                pltpu.make_async_remote_copy(
                    src_ref=back.at[own_rows], dst_ref=home.at[own_rows], send_sem=back_sem,
                    recv_sem=home_sem, device_id=peer(i, -1), device_id_type=MESH,
                ).start()

            return 0

        lax.fori_loop(c * per, (c + 1) * per, give, 0)
        step = 512
        for b in range(width // step):
            cols = slice(b * step, (b + 1) * step)
            mo[:, cols] += mm_tn(hid[...], rows_g[rows, cols])
        return 0

    lax.fori_loop(0, CHUNKS, chunk, 0)

    def squares(b, total):
        part = mo[pl.ds(pl.multiple_of(b * 32, 32), 32), :]
        part = part * part
        return total + jnp.sum(part.reshape(4, 8, width), axis=0)

    norm2 = jnp.sum(lax.fori_loop(0, hidden // 32, squares, jnp.zeros((8, width), F32)))
    inverse = 1.0 / (jnp.sqrt(jnp.full((8, LANES), norm2, F32)) + NORM_EPS)
    inverse = inverse[0:1, 0:1]

    def scaled(b, _):
        rows = pl.ds(pl.multiple_of(b * 64, 64), 64)
        ortho[rows, :] = (mo[rows, :] * inverse).astype(BF)
        return 0

    lax.fori_loop(0, hidden // 64, scaled, 0)

    lin, quad, quart = NS_COEFFS
    step = 512
    for turn in range(NS_STEPS):
        sq[...] = mm_nt(ortho[...], ortho[...]).astype(BF)
        poly[...] = (quad * sq[...].astype(F32) + quart * mm(sq[...], sq[...])).astype(BF)
        scale = math.sqrt(width) if turn + 1 == NS_STEPS else None
        for b in range(width // step):
            cols = slice(b * step, (b + 1) * step)
            mixed = lin * ortho[:, cols].astype(F32) + mm(poly[...], ortho[:, cols])
            ortho[:, cols] = (mixed if scale is None else scale * mixed).astype(BF)

    step = 2 * LANES

    def weight_grads(b, _):
        rows = pl.ds(pl.multiple_of(b * step, step), step)
        x = rows_x[:, rows]
        gg_v[rows, :] = mm_tn(x, ggp[...]).astype(BF)
        gu_v[rows, :] = mm_tn(x, gup[...]).astype(BF)
        return 0

    lax.fori_loop(0, width // step, weight_grads, 0)
    pltpu.make_async_copy(home, home, home_sem).wait()
    rest = pl.ds(1, n - 1)
    pltpu.make_async_copy(send.at[rest], send.at[rest], send_sem).wait()
    rest = pl.ds(CAP, (n - 1) * CAP)
    pltpu.make_async_copy(back.at[rest], back.at[rest], back_sem).wait()


def finish(
    place, home, mo, ortho, gg_v, gu_v,
    gi_out, gg_out, gu_out, mo_out, upd_out,
    place_of, sums, gi, store_sem, place_sem,
):
    toks, subs, _ = sums.shape
    plan = pltpu.make_async_copy(place, place_of, place_sem)
    plan.start()
    stores = []
    for k, (src, dst) in enumerate([(mo, mo_out), (ortho, upd_out), (gg_v, gg_out), (gu_v, gu_out)]):
        part = src.shape[0] // PIECES
        for p in range(PIECES):
            rows = pl.ds(p * part, part)
            stores.append(pltpu.make_async_copy(src.at[rows], dst.at[rows], store_sem.at[k * PIECES + p]))
            stores[-1].start()
    plan.wait()

    def combine(t, _):
        sums[t] = home[place_of[0, t]].astype(F32) + home[place_of[1, t]].astype(F32)
        return 0

    lax.fori_loop(0, toks, combine, 0, unroll=4)
    flat = sums.reshape(toks * subs, LANES)
    for j in range(subs):
        gi[:, j * LANES:(j + 1) * LANES] = flat[pl.ds(j, toks, stride=subs), :].astype(BF)
    stores.append(pltpu.make_async_copy(gi, gi_out, store_sem.at[4 * PIECES]))
    stores[-1].start()
    for s in stores:
        s.wait()


def per_device(tokens, grad_out, routes, route_probs, gate_weight, up_weight, down_weight, momentum):
    wide, eight = lax.axis_size("wide"), lax.axis_size("eight")
    n = wide * eight
    toks = routes.shape[0]
    width = tokens.shape[1]
    hidden = down_weight.shape[1]
    subs = width // LANES
    slots = n * CAP
    vmem = pl.BlockSpec(memory_space=pltpu.VMEM)
    hbm = pl.BlockSpec(memory_space=pl.ANY)
    kept = pl.pallas_call(
        functools.partial(kernel, wide, eight),
        out_shape=(
            jax.ShapeDtypeStruct((8, toks), jnp.int32),
            pltpu.VMEM((slots, subs, LANES), BF),
            pltpu.VMEM((hidden, width), F32),
            pltpu.VMEM((hidden, width), BF),
            pltpu.VMEM((width, hidden), BF),
            pltpu.VMEM((width, hidden), BF),
        ),
        in_specs=[pl.BlockSpec(memory_space=pltpu.HBM)] * 8,
        out_specs=(vmem,) * 6,
        scratch_shapes=[
            pltpu.VMEM((2, toks), jnp.int32),
            pltpu.VMEM((2, toks), F32),
            pltpu.VMEM((toks, width), BF),
            pltpu.VMEM((toks, width), BF),
            pltpu.VMEM((8, n), jnp.int32),
            pltpu.VMEM((8, n), F32),
            pltpu.SMEM((8, n), jnp.int32),
            pltpu.SMEM((8, n), F32),
            pltpu.VMEM((toks, subs, LANES), F32),
            pltpu.VMEM((toks, subs, LANES), F32),
            pltpu.VMEM((n, 2 * CAP, subs, LANES), BF),
            pltpu.VMEM((n, 2 * CAP, subs, LANES), BF),
            pltpu.VMEM((slots, subs, LANES), BF),
            pltpu.VMEM((slots // CHUNKS * subs, LANES), F32),
            pltpu.VMEM((slots, width), BF),
            pltpu.VMEM((slots, width), BF),
            pltpu.VMEM((slots // CHUNKS, hidden), BF),
            pltpu.VMEM((slots, hidden), BF),
            pltpu.VMEM((slots, hidden), BF),
            pltpu.VMEM((width, hidden), BF),
            pltpu.VMEM((width, hidden), BF),
            pltpu.VMEM((hidden, width), BF),
            pltpu.VMEM((hidden, hidden), BF),
            pltpu.VMEM((hidden, hidden), BF),
            pltpu.SemaphoreType.DMA((10,)),
            pltpu.SemaphoreType.DMA,
            pltpu.SemaphoreType.DMA((CHUNKS,)),
            pltpu.SemaphoreType.DMA,
            pltpu.SemaphoreType.DMA,
            pltpu.SemaphoreType.REGULAR,
        ],
        compiler_params=pltpu.CompilerParams(
            collective_id=0, has_side_effects=True, vmem_limit_bytes=40 * 2**20
        ),
        name="experts",
    )(
        *(
            pltpu.with_memory_space_constraint(a, pltpu.HBM)
            for a in (
                routes.T, route_probs.T, tokens, grad_out,
                gate_weight[0], up_weight[0], down_weight[0], momentum[0],
            )
        )
    )
    gi, gg, gu, mo, upd = pl.pallas_call(
        finish,
        out_shape=(
            jax.ShapeDtypeStruct((toks, width), BF),
            jax.ShapeDtypeStruct((width, hidden), BF),
            jax.ShapeDtypeStruct((width, hidden), BF),
            jax.ShapeDtypeStruct((hidden, width), F32),
            jax.ShapeDtypeStruct((hidden, width), BF),
        ),
        in_specs=[vmem] * 6,
        out_specs=(hbm,) * 5,
        scratch_shapes=[
            pltpu.SMEM((8, toks), jnp.int32),
            pltpu.VMEM((toks, subs, LANES), F32),
            pltpu.VMEM((toks, width), BF),
            pltpu.SemaphoreType.DMA((4 * PIECES + 1,)),
            pltpu.SemaphoreType.DMA,
        ],
        compiler_params=pltpu.CompilerParams(vmem_limit_bytes=16 * 2**20),
        name="finish",
    )(*kept)
    return gi, gg[None], gu[None], mo[None], upd[None]


def solution(mesh):
    flat, deep = P(("wide", "eight"), None), P(("wide", "eight"), None, None)
    return jax.shard_map(
        per_device,
        mesh=mesh,
        in_specs=(flat,) * 4 + (deep,) * 4,
        out_specs=(flat,) + (deep,) * 4,
        check_vma=False,
    )
```

```python
import functools
import math

import jax
import jax.numpy as jnp
from jax import lax
from jax.experimental import pallas as pl
from jax.experimental.pallas import tpu as pltpu
from jax.sharding import PartitionSpec as P

MESH = pl.DeviceIdType.MESH
BF = jnp.bfloat16
F32 = jnp.float32
NS_STEPS = 3
NS_COEFFS = (3.4445, -4.775, 2.0315)
DECAY = 0.95
NORM_EPS = 1e-07
CAP = 3
STRIDE = 37
CHUNKS = 4
PIECES = 4
LANES = 128


def axis_dims(size):
    return {16: (4, 4), 8: (4, 2)}.get(size, (size,))


def digits(value, dims):
    out = []
    for d in reversed(dims):
        out.append(lax.rem(value, d))
        value = lax.div(value, d)
    return out[::-1]


def number(parts, dims):
    value = parts[0]
    for p, d in zip(parts[1:], dims[1:]):
        value = value * d + p
    return value


def shifted(place, offset, dims, sign):
    return number(
        [lax.rem(p + d + sign * o, d) for p, o, d in zip(digits(place, dims), digits(offset, dims), dims)],
        dims,
    )


def mm(a, b):
    return lax.dot_general(a, b, (((1,), (0,)), ((), ())), preferred_element_type=F32)


def mm_nt(a, b):
    return lax.dot_general(a, b, (((1,), (1,)), ((), ())), preferred_element_type=F32)


def mm_tn(a, b):
    return lax.dot_general(a, b, (((0,), (0,)), ((), ())), preferred_element_type=F32)


def kernel(
    wide, eight,
    routes_hbm, probs_hbm, tok_hbm, grad_hbm, gate_hbm, up_hbm, down_hbm, mom_hbm,
    place_out, home, mo, ortho, rows_x, ggp, gup,
    routes, probs, tokens, grad_out, tok_v, prob_v, tok_of, prob_of,
    tok_f, grad_f, send, recv, back, tile_f, rows_g, hid,
    gate_w, up_w, down_w, sq, poly,
    load_sem, send_sem, recv_sem, back_sem, home_sem, plane_sem,
):
    n = wide * eight
    toks, width = tokens.shape
    hidden = down_w.shape[0]
    subs = width // LANES
    per = n // CHUNKS
    crows = per * CAP
    me = (lax.axis_index("wide"), lax.axis_index("eight"))
    wd, ed = axis_dims(wide), axis_dims(eight)

    def peer(block, sign):
        o = lax.rem(block * STRIDE, n)
        return (
            shifted(me[0], lax.div(o, eight), wd, sign),
            shifted(me[1], lax.rem(o, eight), ed, sign),
        )

    def across(i):
        return lax.rem(me[0] + i, wide), me[1]

    def along(i):
        return me[0], lax.rem(me[1] + i, eight)

    loads = [
        pltpu.make_async_copy(src, dst, load_sem.at[k])
        for k, (src, dst) in enumerate(
            [
                (routes_hbm, routes), (probs_hbm, probs), (tok_hbm, tokens), (grad_hbm, grad_out),
                (gate_hbm, gate_w), (up_hbm, up_w), (down_hbm, down_w), (mom_hbm, mo),
            ]
        )
    ]
    for c in loads[:4]:
        c.start()

    barrier = pltpu.get_barrier_semaphore()
    for sem, size, there in ((barrier, wide, across), (barrier, eight, along)):
        for i in range(1, size):
            pl.semaphore_signal(sem, inc=1, device_id=there(i), device_id_type=MESH)
    for c in loads[4:]:
        c.start()

    loads[0].wait()
    loads[1].wait()

    def block_of(e):
        there = (e >> (eight.bit_length() - 1), e & (eight - 1))
        o, shift = jnp.zeros_like(e), 0
        for part, here, dims in zip(there[::-1], me[::-1], (ed, wd)):
            for d, h in zip(dims[::-1], digits(here, dims)[::-1]):
                o = o + (((part - h) & (d - 1)) << shift)
                shift += d.bit_length() - 1
                part = part >> (d.bit_length() - 1)
        return (o * pow(STRIDE, -1, n)) & (n - 1)

    def down(line):
        return jnp.broadcast_to(line, (toks, toks)).T

    sub = lax.broadcasted_iota(jnp.int32, (toks, toks), 0)
    lane = lax.broadcasted_iota(jnp.int32, (toks, toks), 1)
    e0, e1 = routes[0:1, :], routes[1:2, :]
    c0, c1 = down(e0), down(e1)

    def count(mask):
        return jnp.sum(jnp.where(mask, 1, 0), axis=0, keepdims=True)

    rank0 = count((c0 == e0) & (sub < lane))
    rank1 = count(c0 == e1) + count((c1 == e1) & (sub < lane))
    b0, b1 = block_of(e0), block_of(e1)
    place_out[0:1, :] = b0 * CAP + rank0
    place_out[1:2, :] = b1 * CAP + rank1
    p0, p1 = down(rank0 * n + b0), down(rank1 * n + b1)
    w0, w1 = down(probs[0:1, :]), down(probs[1:2, :])
    if n != toks:
        p0, p1, w0, w1 = (jnp.broadcast_to(v[:, :1], (toks, n)) for v in (p0, p1, w0, w1))
    sub = lax.broadcasted_iota(jnp.int32, (toks, n), 0)
    lane = lax.broadcasted_iota(jnp.int32, (toks, n), 1)
    for s in range(CAP):
        m0, m1 = p0 == lane + s * n, p1 == lane + s * n
        tok_v[s:s + 1, :] = jnp.sum(jnp.where(m0 | m1, sub, 0), axis=0, keepdims=True)
        prob_v[s:s + 1, :] = jnp.sum(
            jnp.where(m0, w0, 0.0) + jnp.where(m1, w1, 0.0), axis=0, keepdims=True
        )
    maps = [
        pltpu.make_async_copy(src, dst, load_sem.at[len(loads) + k])
        for k, (src, dst) in enumerate([(tok_v, tok_of), (prob_v, prob_of)])
    ]
    for c in maps:
        c.start()

    pl.semaphore_wait(barrier, wide + eight - 2)
    for i in range(1, eight):
        pl.semaphore_signal(plane_sem, inc=1, device_id=along(i), device_id_type=MESH)
    loads[2].wait()
    loads[3].wait()

    tok_flat, grad_flat = (r.reshape(toks * subs, LANES) for r in (tok_f, grad_f))
    for j in range(subs):
        cols = slice(j * LANES, (j + 1) * LANES)
        tok_flat[pl.ds(j, toks, stride=subs), :] = tokens[:, cols].astype(F32)
        grad_flat[pl.ds(j, toks, stride=subs), :] = grad_out[:, cols].astype(F32)

    def fill(i):
        for s in range(CAP):
            token = tok_of[s, i]
            send[i, s] = tok_f[token].astype(BF)
            send[i, CAP + s] = (prob_of[s, i] * grad_f[token]).astype(BF)

    for c in maps:
        c.wait()
    fill(0)
    own = pltpu.make_async_copy(send.at[0], recv.at[0], recv_sem.at[0])
    own.start()

    pl.semaphore_wait(plane_sem, eight - 1)

    def dispatch(i, _):
        fill(i)
        pltpu.make_async_remote_copy(
            src_ref=send.at[i], dst_ref=recv.at[i], send_sem=send_sem,
            recv_sem=recv_sem.at[lax.div(i, per)], device_id=peer(i, 1), device_id_type=MESH,
        ).start()
        return 0

    lax.fori_loop(1, n, dispatch, 0)

    for c in loads[4:]:
        c.wait()

    def decay(b, _):
        rows = pl.ds(pl.multiple_of(b * 64, 64), 64)
        mo[rows, :] = DECAY * mo[rows, :]
        return 0

    lax.fori_loop(0, hidden // 64, decay, 0)

    def chunk(c, _):
        blocks = pl.ds(c * per, per)
        rows = pl.ds(pl.multiple_of(c * crows, crows), crows)
        pltpu.make_async_copy(recv.at[blocks], recv.at[blocks], recv_sem.at[c]).wait()
        for part, dest in ((0, rows_x), (CAP, rows_g)):
            tile_f[...] = recv[blocks, part:part + CAP].astype(F32).reshape(crows * subs, LANES)
            for j in range(subs):
                dest[rows, j * LANES:(j + 1) * LANES] = tile_f[pl.ds(j, crows, stride=subs), :].astype(BF)
        x, g = rows_x[rows, :], rows_g[rows, :]
        gate_pre = mm(x, gate_w[...])
        upper = mm(x, up_w[...])
        grad_hidden = mm_nt(g, down_w[...])
        sig = jax.nn.sigmoid(gate_pre)
        act = gate_pre * sig
        slope = sig * (1.0 + gate_pre * (1.0 - sig))
        hid[...] = (act * upper).astype(BF)
        ggp[rows, :] = (grad_hidden * upper * slope).astype(BF)
        gup[rows, :] = (grad_hidden * act).astype(BF)
        step = 2 * LANES
        for b in range(width // step):
            cols = slice(b * step, (b + 1) * step)
            gr = mm_nt(ggp[rows, :], gate_w[cols, :]) + mm_nt(gup[rows, :], up_w[cols, :])
            tile_f[pl.ds(2 * b, crows, stride=subs), :] = gr[:, :LANES]
            tile_f[pl.ds(2 * b + 1, crows, stride=subs), :] = gr[:, LANES:]
        back[rows] = tile_f[...].astype(BF).reshape(crows, subs, LANES)

        def give(i, _):
            own_rows = pl.ds(i * CAP, CAP)

            @pl.when(i == 0)
            def _():
                pltpu.make_async_copy(back.at[own_rows], home.at[own_rows], home_sem).start()

            @pl.when(i > 0)
            def _():
                pltpu.make_async_remote_copy(
                    src_ref=back.at[own_rows], dst_ref=home.at[own_rows], send_sem=back_sem,
                    recv_sem=home_sem, device_id=peer(i, -1), device_id_type=MESH,
                ).start()

            return 0

        lax.fori_loop(c * per, (c + 1) * per, give, 0)
        step = 512
        for b in range(width // step):
            cols = slice(b * step, (b + 1) * step)
            mo[:, cols] += mm_tn(hid[...], rows_g[rows, cols])
        return 0

    lax.fori_loop(0, CHUNKS, chunk, 0)

    def squares(b, total):
        part = mo[pl.ds(pl.multiple_of(b * 32, 32), 32), :]
        part = part * part
        return total + jnp.sum(part.reshape(4, 8, width), axis=0)

    norm2 = jnp.sum(lax.fori_loop(0, hidden // 32, squares, jnp.zeros((8, width), F32)))
    inverse = 1.0 / (jnp.sqrt(jnp.full((8, LANES), norm2, F32)) + NORM_EPS)
    inverse = inverse[0:1, 0:1]

    def scaled(b, _):
        rows = pl.ds(pl.multiple_of(b * 64, 64), 64)
        ortho[rows, :] = (mo[rows, :] * inverse).astype(BF)
        return 0

    lax.fori_loop(0, hidden // 64, scaled, 0)

    lin, quad, quart = NS_COEFFS
    step = 512
    for turn in range(NS_STEPS):
        sq[...] = mm_nt(ortho[...], ortho[...]).astype(BF)
        poly[...] = (quad * sq[...].astype(F32) + quart * mm(sq[...], sq[...])).astype(BF)
        scale = math.sqrt(width) if turn + 1 == NS_STEPS else None
        for b in range(width // step):
            cols = slice(b * step, (b + 1) * step)
            mixed = lin * ortho[:, cols].astype(F32) + mm(poly[...], ortho[:, cols])
            ortho[:, cols] = (mixed if scale is None else scale * mixed).astype(BF)

    pltpu.make_async_copy(home, home, home_sem).wait()
    rest = pl.ds(1, n - 1)
    pltpu.make_async_copy(send.at[rest], send.at[rest], send_sem).wait()
    rest = pl.ds(CAP, (n - 1) * CAP)
    pltpu.make_async_copy(back.at[rest], back.at[rest], back_sem).wait()


def finish(
    place, home, mo, ortho, rows_x, ggp, gup,
    gi_out, gg_out, gu_out, mo_out, upd_out,
    place_of, sums, gi, gg_v, gu_v, store_sem, grad_sem, place_sem,
):
    toks, subs, _ = sums.shape
    plan = pltpu.make_async_copy(place, place_of, place_sem)
    plan.start()
    stores = []
    for k, (src, dst) in enumerate([(mo, mo_out), (ortho, upd_out)]):
        part = src.shape[0] // PIECES
        for p in range(PIECES):
            rows = pl.ds(p * part, part)
            stores.append(pltpu.make_async_copy(src.at[rows], dst.at[rows], store_sem.at[k * PIECES + p]))
            stores[-1].start()
    plan.wait()

    def combine(t, _):
        sums[t] = home[place_of[0, t]].astype(F32) + home[place_of[1, t]].astype(F32)
        return 0

    lax.fori_loop(0, toks, combine, 0, unroll=4)
    flat = sums.reshape(toks * subs, LANES)
    for j in range(subs):
        gi[:, j * LANES:(j + 1) * LANES] = flat[pl.ds(j, toks, stride=subs), :].astype(BF)
    stores.append(pltpu.make_async_copy(gi, gi_out, store_sem.at[2 * PIECES]))
    stores[-1].start()
    step = 2 * LANES
    for b in range(gg_v.shape[0] // step):
        rows = pl.ds(b * step, step)
        x = rows_x[:, b * step:(b + 1) * step]
        for k, (grad, held, out) in enumerate([(ggp, gg_v, gg_out), (gup, gu_v, gu_out)]):
            held[rows, :] = mm_tn(x, grad[...]).astype(BF)
            stores.append(pltpu.make_async_copy(held.at[rows], out.at[rows], grad_sem.at[2 * b + k]))
            stores[-1].start()
    for s in stores:
        s.wait()


def per_device(tokens, grad_out, routes, route_probs, gate_weight, up_weight, down_weight, momentum):
    wide, eight = lax.axis_size("wide"), lax.axis_size("eight")
    n = wide * eight
    toks = routes.shape[0]
    width = tokens.shape[1]
    hidden = down_weight.shape[1]
    subs = width // LANES
    slots = n * CAP
    vmem = pl.BlockSpec(memory_space=pltpu.VMEM)
    hbm = pl.BlockSpec(memory_space=pl.ANY)
    kept = pl.pallas_call(
        functools.partial(kernel, wide, eight),
        out_shape=(
            jax.ShapeDtypeStruct((8, toks), jnp.int32),
            pltpu.VMEM((slots, subs, LANES), BF),
            pltpu.VMEM((hidden, width), F32),
            pltpu.VMEM((hidden, width), BF),
            pltpu.VMEM((slots, width), BF),
            pltpu.VMEM((slots, hidden), BF),
            pltpu.VMEM((slots, hidden), BF),
        ),
        in_specs=[pl.BlockSpec(memory_space=pltpu.HBM)] * 8,
        out_specs=(vmem,) * 7,
        scratch_shapes=[
            pltpu.VMEM((2, toks), jnp.int32),
            pltpu.VMEM((2, toks), F32),
            pltpu.VMEM((toks, width), BF),
            pltpu.VMEM((toks, width), BF),
            pltpu.VMEM((8, n), jnp.int32),
            pltpu.VMEM((8, n), F32),
            pltpu.SMEM((8, n), jnp.int32),
            pltpu.SMEM((8, n), F32),
            pltpu.VMEM((toks, subs, LANES), F32),
            pltpu.VMEM((toks, subs, LANES), F32),
            pltpu.VMEM((n, 2 * CAP, subs, LANES), BF),
            pltpu.VMEM((n, 2 * CAP, subs, LANES), BF),
            pltpu.VMEM((slots, subs, LANES), BF),
            pltpu.VMEM((slots // CHUNKS * subs, LANES), F32),
            pltpu.VMEM((slots, width), BF),
            pltpu.VMEM((slots // CHUNKS, hidden), BF),
            pltpu.VMEM((width, hidden), BF),
            pltpu.VMEM((width, hidden), BF),
            pltpu.VMEM((hidden, width), BF),
            pltpu.VMEM((hidden, hidden), BF),
            pltpu.VMEM((hidden, hidden), BF),
            pltpu.SemaphoreType.DMA((10,)),
            pltpu.SemaphoreType.DMA,
            pltpu.SemaphoreType.DMA((CHUNKS,)),
            pltpu.SemaphoreType.DMA,
            pltpu.SemaphoreType.DMA,
            pltpu.SemaphoreType.REGULAR,
        ],
        compiler_params=pltpu.CompilerParams(
            collective_id=0, has_side_effects=True, vmem_limit_bytes=40 * 2**20
        ),
        name="experts",
    )(
        *(
            pltpu.with_memory_space_constraint(a, pltpu.HBM)
            for a in (
                routes.T, route_probs.T, tokens, grad_out,
                gate_weight[0], up_weight[0], down_weight[0], momentum[0],
            )
        )
    )
    gi, gg, gu, mo, upd = pl.pallas_call(
        finish,
        out_shape=(
            jax.ShapeDtypeStruct((toks, width), BF),
            jax.ShapeDtypeStruct((width, hidden), BF),
            jax.ShapeDtypeStruct((width, hidden), BF),
            jax.ShapeDtypeStruct((hidden, width), F32),
            jax.ShapeDtypeStruct((hidden, width), BF),
        ),
        in_specs=[vmem] * 7,
        out_specs=(hbm,) * 5,
        scratch_shapes=[
            pltpu.SMEM((8, toks), jnp.int32),
            pltpu.VMEM((toks, subs, LANES), F32),
            pltpu.VMEM((toks, width), BF),
            pltpu.VMEM((width, hidden), BF),
            pltpu.VMEM((width, hidden), BF),
            pltpu.SemaphoreType.DMA((2 * PIECES + 1,)),
            pltpu.SemaphoreType.DMA((2 * width // (2 * LANES),)),
            pltpu.SemaphoreType.DMA,
        ],
        compiler_params=pltpu.CompilerParams(vmem_limit_bytes=16 * 2**20),
        name="finish",
    )(*kept)
    return gi, gg[None], gu[None], mo[None], upd[None]


def solution(mesh):
    flat, deep = P(("wide", "eight"), None), P(("wide", "eight"), None, None)
    return jax.shard_map(
        per_device,
        mesh=mesh,
        in_specs=(flat,) * 4 + (deep,) * 4,
        out_specs=(flat,) + (deep,) * 4,
        check_vma=False,
    )
```
